32 devices in a mesh: groups: 2 (over x), docs: 8 (over z, y), mods: 2 (over core).
Axes of the slice: x: 2, y: 2, z: 4, core: 2. Of those that a mesh axis runs over, the one named last changes fastest.
Arguments:
- doc_grads: bfloat16 [16384, 24576], P(('groups', 'docs'), 'mods'), parts along dimension 0, may hold values from -6 to 6
- query_grads: bfloat16 [512, 24576], P(('groups', 'docs'), 'mods'), parts along dimension 0, may hold values from -6 to 6
- basis_in: float32 [6, 64, 64], P('mods'), may hold values from -0.75 to 0.75
- basis_out: float32 [6, 64, 64], P('mods'), may hold values from -0.75 to 0.75
- eigen: float32 [6, 64, 64], P('mods'), may hold values from 0.05 to 20
- token_counts: int32 [16384], P(('groups', 'docs')), parts along dimension 0, may hold values from 512 to 2048
Outputs:
- influence: float32 [16384, 256], P(('groups', 'docs')), parts along dimension 0
The draws below stay inside these ranges and needn't reach their ends.
There are 2 independent parts, one for each index of `groups`. The reference program is written for one: setup_inputs(seed, part) draws one part's arguments, and reference() takes and returns one part's arrays. A program takes and returns all parts, laid end to end along the dimension named above; an argument that names none is the same for every part. Nothing has to cross between parts.
All inputs are finite; a program needn't handle non-finite values.
Results may differ from the reference program's by a relative error of at most 0.008.
Values may be sent and summed in bfloat16 or wider, within the bound.
A program may use at most 128 MiB of HBM per device.

```python
import math
import jax
import jax.numpy as jnp
from jax import lax

K = 64
MODULES = 6
FEAT = 24576
QUERIES = 256
DOCS = 8192


def plant(values, key, least, high):
    longest = values.shape.index(max(values.shape))
    spots = []
    for shift in (0, 1):
        where = [jax.random.randint(jax.random.fold_in(key, axis), (), 0, length) for axis, length in enumerate(values.shape)]
        where[longest] = (where[longest] + shift) % values.shape[longest]
        spots.append(tuple(where))
    return values.at[spots[0]].set(least).at[spots[1]].set(high)


def shard_levels(key, shape, cuts, least, high):
    loudness, own = 1.0, jax.random.fold_in(key, 6)
    for dim, blocks in cuts:
        draws = jnp.exp(jax.random.uniform(jax.random.fold_in(own, dim), (blocks,), jnp.float32, least / len(cuts), high / len(cuts)))
        loudness = loudness * jnp.repeat(draws, shape[dim] // blocks).reshape([-1 if axis == dim else 1 for axis in range(len(shape))])
    return loudness


def bell_draw(own_key, shape, scale, reach, cuts=(), held_as=jnp.bfloat16):
    loudness = shard_levels(own_key, shape, cuts, -0.22, 0.18) if cuts else 1.0
    result = jax.random.normal(own_key, shape, jnp.float32) * scale * loudness
    return jnp.minimum(jnp.maximum(result, -reach), reach).astype(held_as)


def setup_inputs(seed: int = 0, part: int = 0) -> dict:
    key_of = jax.random.split(jax.random.key(seed), 7)
    part_splits = jax.random.split(jax.random.fold_in(key_of[6], part), 7)
    return {
        "doc_grads": bell_draw(part_splits[0], (DOCS, FEAT), 1.0, 6.0, ((0, 8), (1, 2))),
        "query_grads": bell_draw(part_splits[1], (QUERIES, FEAT), 1.0, 6.0, ((0, 8), (1, 2))),
        "basis_in": bell_draw(key_of[2], (MODULES, K, K), K ** -0.5, 0.75, ((0, 2),), jnp.float32),
        "basis_out": bell_draw(key_of[3], (MODULES, K, K), K ** -0.5, 0.75, ((0, 2),), jnp.float32),
        "eigen": jnp.clip(jnp.exp(math.log(20.0) - 5.9914645 * jax.random.uniform(key_of[4], (MODULES, K, K), jnp.float32) ** shard_levels(key_of[4], (MODULES, K, K), ((0, 2),), -0.2, 0.2)), 0.05, 20.0),
        "token_counts": plant(jax.random.randint(part_splits[5], (DOCS,), 512, 2049), jax.random.fold_in(part_splits[5], 1), 512, 2048).astype(jnp.int32),
    }


ref_tokens = 1024.0

def precondition(gradient, basis_in, basis_out, eigen):
    high = lax.Precision.HIGHEST
    rotated = jnp.einsum('qmab,mai->qmib', gradient, basis_in, precision=high)
    rotated = jnp.einsum('qmib,mbj->qmij', rotated, basis_out, precision=high)
    damping = 0.1 * lax.optimization_barrier(jnp.mean(eigen, axis=(1, 2)))
    scaled = rotated / (eigen + damping[:, None, None])
    mapped = jnp.einsum('qmij,mbj->qmib', scaled, basis_out, precision=high)
    mapped = jnp.einsum('qmib,mai->qmab', mapped, basis_in, precision=high)
    self_score = lax.optimization_barrier(jnp.sum(gradient * mapped, axis=(1, 2, 3)))
    return (mapped, self_score)

def reference(doc_grads, query_grads, basis_in, basis_out, eigen, token_counts):
    gradient = query_grads.reshape(QUERIES, MODULES, K, K).astype(jnp.float32)
    mapped, self_score = precondition(gradient, basis_in, basis_out, eigen)
    precond = mapped.reshape(QUERIES, FEAT).astype(jnp.bfloat16)
    raw = lax.dot_general(doc_grads, precond, (((1,), (1,)), ((), ())), preferred_element_type=jnp.float32)
    factor = ref_tokens / token_counts.astype(jnp.float32)
    return raw / jnp.sqrt(self_score)[None, :] * factor[:, None]
```

```python
import jax
import jax.numpy as jnp
from jax import lax
from jax.sharding import PartitionSpec as P

ref_tokens = 1024.0
bf16, f32 = jnp.bfloat16, jnp.float32


def precondition(gradient, basis_in, basis_out, eigen):
    high = lax.Precision.HIGH
    rotated = jnp.einsum("qab,bj->qaj", gradient, basis_out, precision=high)
    rotated = jnp.einsum("qaj,ai->qij", rotated, basis_in, precision=high)
    damping = 0.1 * jnp.mean(eigen)
    scaled = rotated / (eigen + damping)
    self_score = jnp.sum(rotated * scaled, axis=(1, 2))
    mapped = jnp.einsum("qij,ai->qaj", scaled, basis_in, precision=high)
    mapped = jnp.einsum("qaj,bj->qab", mapped, basis_out, precision=high)
    return mapped, self_score


def shards(doc_grads, query_grads, basis_in, basis_out, eigen, token_counts):
    queries_here = query_grads.shape[0]
    mods_here = basis_in.shape[0]
    width = basis_in.shape[1]
    size = width * width
    mods = lax.axis_size("mods")
    me_mod = lax.axis_index("mods")
    self_part = jnp.zeros((queries_here,), f32)
    scores = None
    for m in range(mods_here):
        gradient = query_grads[:, m * size : (m + 1) * size]
        gradient = gradient.reshape(queries_here, width, width).astype(f32)
        mapped, self_m = precondition(gradient, basis_in[m], basis_out[m], eigen[m])
        self_part = self_part + self_m
        block = mapped.reshape(queries_here, size).astype(bf16)
        if m == mods_here - 1:
            upper = self_part.astype(bf16)
            lower = (self_part - upper.astype(f32)).astype(bf16)
            pair = jnp.pad(jnp.stack([upper, lower], axis=1), ((0, 0), (0, 126)))
            block = jnp.concatenate([block, pair], axis=1)
        every = lax.all_gather(block, "docs", axis=0, tiled=True)
        part = lax.dot_general(
            doc_grads[:, m * size : (m + 1) * size],
            every[:, :size],
            (((1,), (1,)), ((), ())),
            preferred_element_type=f32,
        )
        scores = part if scores is None else scores + part
    pair = every[:, size : size + 2].T
    rows = [jnp.where(me_mod == k, pair, jnp.zeros_like(pair)) for k in range(mods)]
    totals = lax.psum(jnp.concatenate([scores.astype(bf16)] + rows, axis=0), "mods")
    docs_here = doc_grads.shape[0]
    self_terms = jnp.sum(totals[docs_here:].astype(f32), axis=0)
    factor = ref_tokens / token_counts.astype(f32)
    return totals[:docs_here].astype(f32) * lax.rsqrt(self_terms)[None, :] * factor[:, None]


def solution(mesh):
    in_specs = (
        P(("groups", "docs"), "mods"),
        P(("groups", "docs"), "mods"),
        P("mods", None, None),
        P("mods", None, None),
        P("mods", None, None),
        P(("groups", "docs")),
    )
    out_specs = P(("groups", "docs"), None)
    return jax.shard_map(shards, mesh=mesh, in_specs=in_specs, out_specs=out_specs, check_vma=False)
```

```python
import functools

import jax
import jax.numpy as jnp
from jax import lax
from jax.experimental import pallas as pl
from jax.experimental.pallas import tpu as pltpu
from jax.sharding import PartitionSpec as P

ref_tokens = 1024.0
bf16, f32 = jnp.bfloat16, jnp.float32
MESH = pl.DeviceIdType.MESH
NT = (((1,), (1,)), ((), ()))


def precondition(gradient, basis_in, basis_out, eigen):
    high = lax.Precision.HIGH
    rotated = jnp.einsum("qab,bj->qaj", gradient, basis_out, precision=high)
    rotated = jnp.einsum("qaj,ai->qij", rotated, basis_in, precision=high)
    damping = 0.1 * jnp.mean(eigen)
    scaled = rotated / (eigen + damping)
    self_score = jnp.sum(rotated * scaled, axis=(1, 2))
    mapped = jnp.einsum("qij,ai->qaj", scaled, basis_in, precision=high)
    mapped = jnp.einsum("qaj,bj->qab", mapped, basis_out, precision=high)
    return mapped, self_score


def kernel(
    n, pair, chunks, tiles, blk, docs, factor, out, got, docs_v, acc, mine, theirs, selfs,
    their_selfs, send_sem, recv_sem, doc_sem, ex_send, ex_recv,
):
    me = lax.axis_index("docs")
    core = lax.axis_index("mods")
    z = lax.div(me, pair)
    y = lax.rem(me, pair)
    depth = n // pair
    up, down = me + pair, me - pair
    beside = z * pair + (pair - 1 - y)
    has_up, has_down = z < depth - 1, z > 0
    q = blk.shape[0]
    wide = blk.shape[1]
    features = docs.shape[1]
    part = features // chunks
    tile = docs.shape[0] // tiles

    def load(c):
        cols = pl.ds(c * part, part)
        return pltpu.make_async_copy(docs.at[:, cols], docs_v.at[:, cols], doc_sem.at[c])

    for c in range(chunks):
        load(c).start()

    barrier = pltpu.get_barrier_semaphore()
    for yes, to in ((has_up, up), (has_down, down)):

        @pl.when(yes)
        def _(to=to):
            pl.semaphore_signal(barrier, inc=1, device_id={"docs": to}, device_id_type=MESH)

    if pair > 1:
        pl.semaphore_signal(barrier, inc=1, device_id={"docs": beside}, device_id_type=MESH)
    pl.semaphore_signal(barrier, inc=1, device_id={"mods": 1 - core}, device_id_type=MESH)
    peers = 2 if pair > 1 else 1
    line_peers = has_up.astype(jnp.int32) + has_down.astype(jnp.int32)
    pl.semaphore_wait(barrier, peers + line_peers)

    def piece(source, c):
        start = c * part
        stop = (c + 1) * part if c < chunks - 1 else wide
        return (pl.ds(pl.multiple_of(source * q, q), q), pl.ds(start, stop - start))

    def copy(way, source, c, own=False):
        rows, cols = piece(source, c)
        to = (up, down, beside)[way]
        return pltpu.make_async_remote_copy(
            src_ref=blk.at[:, cols] if own else got.at[rows, cols],
            dst_ref=got.at[rows, cols],
            send_sem=send_sem.at[way, source, c],
            recv_sem=recv_sem.at[source, c],
            device_id={"docs": to},
            device_id_type=MESH,
        )

    def own_each(c, act):
        @pl.when(has_up)
        def _():
            act(copy(0, me, c, True))

        @pl.when(has_down)
        def _():
            act(copy(1, me, c, True))

        if pair > 1:
            act(copy(2, me, c, True))

    def line_each(c, wait):
        for d in range(1, depth):

            @pl.when(z >= d)
            def _():
                source = me - d * pair
                if wait:
                    copy(0, source, c).wait_recv()

                @pl.when(has_up)
                def _():
                    one = copy(0, source, c)
                    one.start() if wait else one.wait_send()

                if pair > 1:
                    one = copy(2, source, c)
                    one.start() if wait else one.wait_send()

            @pl.when(z + d < depth)
            def _():
                source = me + d * pair
                if wait:
                    copy(1, source, c).wait_recv()

                @pl.when(has_down)
                def _():
                    one = copy(1, source, c)
                    one.start() if wait else one.wait_send()

                if pair > 1:
                    one = copy(2, source, c)
                    one.start() if wait else one.wait_send()

    def beside_wait(c):
        if pair > 1:
            for level in range(depth):
                copy(2, level * pair + (pair - 1 - y), c).wait_recv()

    def product(c, t):
        rows = pl.ds(t * tile, tile)
        cols = pl.ds(c * part, part)
        value = lax.dot_general(docs_v[rows, cols], got[:, cols], NT, preferred_element_type=f32)
        if c == 0:
            acc[rows, :] = value
            return value
        return acc[rows, :] + value

    for c in range(min(2, chunks)):
        own_each(c, lambda one: one.start())
    got[pl.ds(pl.multiple_of(me * q, q), q), :] = blk[...]
    for c in range(chunks):
        line_each(c, True)
        if c + 2 < chunks:
            own_each(c + 2, lambda one: one.start())
        if c >= 1:
            beside_wait(c - 1)
            load(c - 1).wait()
            for t in range(tiles):
                value = product(c - 1, t)
                if c > 1:
                    acc[pl.ds(t * tile, tile), :] = value

    last = chunks - 1
    beside_wait(last)
    load(last).wait()

    def swap(t):
        if t == tiles:
            src, dst = selfs, their_selfs
        else:
            rows = pl.ds(t * tile, tile)
            src, dst = mine.at[rows, :], theirs.at[rows, :]
        return pltpu.make_async_remote_copy(
            src_ref=src,
            dst_ref=dst,
            send_sem=ex_send.at[t],
            recv_sem=ex_recv.at[t],
            device_id={"mods": 1 - core},
            device_id_type=MESH,
        )

    lane = lax.broadcasted_iota(jnp.int32, (16, wide - features), 1)
    pick = jnp.where(lane < 2, 1.0, 0.0).astype(bf16)
    selfs[...] = lax.dot_general(
        pick, got[:, pl.ds(features, wide - features)], NT, preferred_element_type=f32
    )
    swap(tiles).start()
    for t in range(tiles):
        mine[pl.ds(t * tile, tile), :] = product(last, t).astype(bf16)
        swap(t).start()
    swap(tiles).wait()
    scale = lax.rsqrt(selfs[0:1, :] + their_selfs[0:1, :])
    for t in range(tiles):
        rows = pl.ds(t * tile, tile)
        swap(t).wait()
        total = mine[rows, :].astype(f32) + theirs[rows, :].astype(f32)
        out[rows, :] = total * scale * factor[rows, :]
    for c in range(chunks):
        own_each(c, lambda one: one.wait_send())
        line_each(c, False)


def gather_and_score(n, pair, chunks, block, docs, factor):
    q, wide = block.shape
    rows, features = docs.shape
    queries, tiles = n * q, 4
    vmem = pl.BlockSpec(memory_space=pltpu.VMEM)
    return pl.pallas_call(
        functools.partial(kernel, n, pair, chunks, tiles),
        out_shape=jax.ShapeDtypeStruct((rows, queries), f32),
        in_specs=[vmem, pl.BlockSpec(memory_space=pl.ANY), vmem],
        out_specs=vmem,
        scratch_shapes=[
            pltpu.VMEM((queries, wide), bf16),
            pltpu.VMEM((rows, features), bf16),
            pltpu.VMEM((rows, queries), f32),
            pltpu.VMEM((rows, queries), bf16),
            pltpu.VMEM((rows, queries), bf16),
            pltpu.VMEM((16, queries), f32),
            pltpu.VMEM((16, queries), f32),
            pltpu.SemaphoreType.DMA((3, n, chunks)),
            pltpu.SemaphoreType.DMA((n, chunks)),
            pltpu.SemaphoreType.DMA((chunks,)),
            pltpu.SemaphoreType.DMA((tiles + 1,)),
            pltpu.SemaphoreType.DMA((tiles + 1,)),
        ],
        compiler_params=pltpu.CompilerParams(
            collective_id=0, has_side_effects=True, vmem_limit_bytes=52 << 20
        ),
        cost_estimate=pl.CostEstimate(
            flops=2 * rows * features * queries,
            bytes_accessed=2 * rows * features,
            transcendentals=0,
        ),
    )(block, docs, factor)


def shards(n, pair, doc_grads, query_grads, basis_in, basis_out, eigen, token_counts):
    queries_here = query_grads.shape[0]
    mods_here = basis_in.shape[0]
    width = basis_in.shape[1]
    size = width * width
    self_part = jnp.zeros((queries_here,), f32)
    blocks = []
    for m in range(mods_here):
        gradient = query_grads[:, m * size : (m + 1) * size]
        gradient = gradient.reshape(queries_here, width, width).astype(f32)
        mapped, self_m = precondition(gradient, basis_in[m], basis_out[m], eigen[m])
        self_part = self_part + self_m
        blocks.append(mapped.reshape(queries_here, size).astype(bf16))
    upper = self_part.astype(bf16)
    lower = (self_part - upper.astype(f32)).astype(bf16)
    blocks.append(jnp.pad(jnp.stack([upper, lower], axis=1), ((0, 0), (0, 126))))
    block = jnp.concatenate(blocks, axis=1)
    factor = (ref_tokens / token_counts.astype(f32))[:, None]
    return gather_and_score(n, pair, mods_here, block, doc_grads, factor)


def solution(mesh):
    n = mesh.shape["docs"]
    pair = 2 if mesh.shape["groups"] == 2 and n % 2 == 0 else 1
    in_specs = (
        P(("groups", "docs"), "mods"),
        P(("groups", "docs"), "mods"),
        P("mods", None, None),
        P("mods", None, None),
        P("mods", None, None),
        P(("groups", "docs")),
    )
    out_specs = P(("groups", "docs"), None)
    body = functools.partial(shards, n, pair)
    return jax.shard_map(body, mesh=mesh, in_specs=in_specs, out_specs=out_specs, check_vma=False)
```

```python
import functools

import jax
import jax.numpy as jnp
from jax import lax
from jax.experimental import pallas as pl
from jax.experimental.pallas import tpu as pltpu
from jax.sharding import PartitionSpec as P

ref_tokens = 1024.0
bf16, f32 = jnp.bfloat16, jnp.float32
MESH = pl.DeviceIdType.MESH
NT = (((1,), (1,)), ((), ()))


def precondition(gradient, basis_in, basis_out, eigen):
    high = lax.Precision.HIGH
    rotated = jnp.einsum("qab,bj->qaj", gradient, basis_out, precision=high)
    rotated = jnp.einsum("qaj,ai->qij", rotated, basis_in, precision=high)
    damping = 0.1 * jnp.mean(eigen)
    scaled = rotated / (eigen + damping)
    self_score = jnp.sum(rotated * scaled, axis=(1, 2))
    mapped = jnp.einsum("qij,ai->qaj", scaled, basis_in, precision=high)
    mapped = jnp.einsum("qaj,bj->qab", mapped, basis_out, precision=high)
    return mapped, self_score


def kernel(
    n, pair, tiles, blk, docs, factor, out, got, docs_v, acc, mine, theirs, selfs,
    their_selfs, send_sem, recv_sem, doc_sem, ex_send, ex_recv,
):
    me = lax.axis_index("docs")
    core = lax.axis_index("mods")
    z = lax.div(me, pair)
    y = lax.rem(me, pair)
    depth = n // pair
    up, down = me + pair, me - pair
    beside = z * pair + (pair - 1 - y)
    has_up, has_down = z < depth - 1, z > 0
    q = blk.shape[0]
    wide = blk.shape[1]
    features = docs.shape[1]
    third = features // 3
    edges = (0, third, 2 * third, 2 * third + third // 4 * 3, features)
    chunks = len(edges) - 1
    tile = docs.shape[0] // tiles

    def load(c):
        cols = pl.ds(edges[c], edges[c + 1] - edges[c])
        return pltpu.make_async_copy(docs.at[:, cols], docs_v.at[:, cols], doc_sem.at[c])

    for c in range(chunks):
        load(c).start()

    barrier = pltpu.get_barrier_semaphore()
    for yes, to in ((has_up, up), (has_down, down)):

        @pl.when(yes)
        def _(to=to):
            pl.semaphore_signal(barrier, inc=1, device_id={"docs": to}, device_id_type=MESH)

    if pair > 1:
        pl.semaphore_signal(barrier, inc=1, device_id={"docs": beside}, device_id_type=MESH)
    pl.semaphore_signal(barrier, inc=1, device_id={"mods": 1 - core}, device_id_type=MESH)
    peers = 2 if pair > 1 else 1
    line_peers = has_up.astype(jnp.int32) + has_down.astype(jnp.int32)
    pl.semaphore_wait(barrier, peers + line_peers)

    both = pair > 1

    def piece(source, k):
        c = k // 2
        start, stop = edges[c], edges[c + 1] if c < chunks - 1 else wide
        cut = stop - (stop - start) * 5 // 32 // 128 * 128 if both else stop
        start, stop = (start, cut) if k % 2 == 0 else (cut, stop)
        return (pl.ds(pl.multiple_of(source * q, q), q), pl.ds(start, stop - start))

    def copy(way, source, k, own=False):
        rows, cols = piece(source, k)
        to = (up, down, beside)[way]
        return pltpu.make_async_remote_copy(
            src_ref=blk.at[:, cols] if own else got.at[rows, cols],
            dst_ref=got.at[rows, cols],
            send_sem=send_sem.at[way, source, k],
            recv_sem=recv_sem.at[source, k],
            device_id={"docs": to},
            device_id_type=MESH,
        )

    lines = ((has_up, 0), (has_down, 1))

    def act(one, first):
        if first:
            one.start()
        else:
            one.wait_send()

    def own_each(c, first):
        if both:
            act(copy(2, me, 2 * c + 1, True), first)
            act(copy(2, me, 2 * c, True), first)
        for yes, way in lines:

            @pl.when(yes)
            def _(way=way):
                act(copy(way, me, 2 * c, True), first)
                if both:
                    act(copy(way, me, 2 * c + 1, True), first)

    def beside_each(c, first):
        if both:
            if first:
                copy(2, beside, 2 * c + 1).wait_recv()
            for yes, way in lines:

                @pl.when(yes)
                def _(way=way):
                    act(copy(way, beside, 2 * c + 1), first)

    def line_each(c, first):
        beside_each(c, first)
        for d in range(1, depth):
            for (onward, way), here, by in zip(lines, (z >= d, z + d < depth), (-d, d)):

                @pl.when(here)
                def _(onward=onward, way=way, by=by):
                    moves = [(me + by * pair, 2 * c)]
                    if both:
                        moves += [(me + by * pair, 2 * c + 1), (beside + by * pair, 2 * c + 1)]
                    for source, k in moves:
                        if first:
                            copy(way, source, k).wait_recv()

                        @pl.when(onward)
                        def _(source=source, k=k):
                            act(copy(way, source, k), first)

                        if both and k % 2 == 0:
                            act(copy(2, source, k), first)

    def beside_wait(c):
        if both:
            for level in range(depth):
                copy(2, level * pair + (pair - 1 - y), 2 * c).wait_recv()

    def product(c, t):
        rows = pl.ds(t * tile, tile)
        cols = pl.ds(edges[c], edges[c + 1] - edges[c])
        value = lax.dot_general(docs_v[rows, cols], got[:, cols], NT, preferred_element_type=f32)
        if c == 0:
            acc[rows, :] = value
            return value
        return acc[rows, :] + value

    for c in range(min(2, chunks)):
        own_each(c, True)
    got[pl.ds(pl.multiple_of(me * q, q), q), :] = blk[...]
    for c in range(chunks):
        line_each(c, True)
        if c + 2 < chunks:
            own_each(c + 2, True)
        if c >= 1:
            beside_wait(c - 1)
            load(c - 1).wait()
            for t in range(tiles):
                value = product(c - 1, t)
                if c > 1:
                    acc[pl.ds(t * tile, tile), :] = value

    last = chunks - 1
    beside_wait(last)
    load(last).wait()

    def swap(t):
        if t == tiles:
            src, dst = selfs, their_selfs
        else:
            rows = pl.ds(t * tile, tile)
            src, dst = mine.at[rows, :], theirs.at[rows, :]
        return pltpu.make_async_remote_copy(
            src_ref=src,
            dst_ref=dst,
            send_sem=ex_send.at[t],
            recv_sem=ex_recv.at[t],
            device_id={"mods": 1 - core},
            device_id_type=MESH,
        )

    lane = lax.broadcasted_iota(jnp.int32, (16, wide - features), 1)
    pick = jnp.where(lane < 2, 1.0, 0.0).astype(bf16)
    selfs[...] = lax.dot_general(
        pick, got[:, pl.ds(features, wide - features)], NT, preferred_element_type=f32
    )
    swap(tiles).start()
    for t in range(tiles):
        mine[pl.ds(t * tile, tile), :] = product(last, t).astype(bf16)
        swap(t).start()
    swap(tiles).wait()
    scale = lax.rsqrt(selfs[0:1, :] + their_selfs[0:1, :])
    for t in range(tiles):
        rows = pl.ds(t * tile, tile)
        swap(t).wait()
        total = mine[rows, :].astype(f32) + theirs[rows, :].astype(f32)
        out[rows, :] = total * scale * factor[rows, :]
    for c in range(chunks):
        own_each(c, False)
        line_each(c, False)


def gather_and_score(n, pair, block, docs, factor):
    q, wide = block.shape
    rows, features = docs.shape
    queries, tiles = n * q, 4
    vmem = pl.BlockSpec(memory_space=pltpu.VMEM)
    return pl.pallas_call(
        functools.partial(kernel, n, pair, tiles),
        out_shape=jax.ShapeDtypeStruct((rows, queries), f32),
        in_specs=[vmem, pl.BlockSpec(memory_space=pl.ANY), vmem],
        out_specs=vmem,
        scratch_shapes=[
            pltpu.VMEM((queries, wide), bf16),
            pltpu.VMEM((rows, features), bf16),
            pltpu.VMEM((rows, queries), f32),
            pltpu.VMEM((rows, queries), bf16),
            pltpu.VMEM((rows, queries), bf16),
            pltpu.VMEM((16, queries), f32),
            pltpu.VMEM((16, queries), f32),
            pltpu.SemaphoreType.DMA((3, n, 8)),
            pltpu.SemaphoreType.DMA((n, 8)),
            pltpu.SemaphoreType.DMA((4,)),
            pltpu.SemaphoreType.DMA((tiles + 1,)),
            pltpu.SemaphoreType.DMA((tiles + 1,)),
        ],
        compiler_params=pltpu.CompilerParams(
            collective_id=0, has_side_effects=True, vmem_limit_bytes=52 << 20
        ),
        cost_estimate=pl.CostEstimate(
            flops=2 * rows * features * queries,
            bytes_accessed=2 * rows * features,
            transcendentals=0,
        ),
    )(block, docs, factor)


def shards(n, pair, doc_grads, query_grads, basis_in, basis_out, eigen, token_counts):
    queries_here = query_grads.shape[0]
    mods_here = basis_in.shape[0]
    width = basis_in.shape[1]
    size = width * width
    self_part = jnp.zeros((queries_here,), f32)
    blocks = []
    for m in range(mods_here):
        gradient = query_grads[:, m * size : (m + 1) * size]
        gradient = gradient.reshape(queries_here, width, width).astype(f32)
        mapped, self_m = precondition(gradient, basis_in[m], basis_out[m], eigen[m])
        self_part = self_part + self_m
        blocks.append(mapped.reshape(queries_here, size).astype(bf16))
    upper = self_part.astype(bf16)
    lower = (self_part - upper.astype(f32)).astype(bf16)
    blocks.append(jnp.pad(jnp.stack([upper, lower], axis=1), ((0, 0), (0, 126))))
    block = jnp.concatenate(blocks, axis=1)
    factor = (ref_tokens / token_counts.astype(f32))[:, None]
    return gather_and_score(n, pair, block, doc_grads, factor)


def solution(mesh):
    n = mesh.shape["docs"]
    pair = 2 if mesh.shape["groups"] == 2 and n % 2 == 0 else 1
    in_specs = (
        P(("groups", "docs"), "mods"),
        P(("groups", "docs"), "mods"),
        P("mods", None, None),
        P("mods", None, None),
        P("mods", None, None),
        P(("groups", "docs")),
    )
    out_specs = P(("groups", "docs"), None)
    body = functools.partial(shards, n, pair)
    return jax.shard_map(body, mesh=mesh, in_specs=in_specs, out_specs=out_specs, check_vma=False)
```

```python
import functools

import jax
import jax.numpy as jnp
from jax import lax
from jax.experimental import pallas as pl
from jax.experimental.pallas import tpu as pltpu
from jax.sharding import PartitionSpec as P

ref_tokens = 1024.0
bf16, f32 = jnp.bfloat16, jnp.float32
MESH = pl.DeviceIdType.MESH
NT = (((1,), (1,)), ((), ()))


def precondition(gradient, basis_in, basis_out, eigen):
    high = lax.Precision.HIGH
    rotated = jnp.einsum("qab,bj->qaj", gradient, basis_out, precision=high)
    rotated = jnp.einsum("qaj,ai->qij", rotated, basis_in, precision=high)
    damping = 0.1 * jnp.mean(eigen)
    scaled = rotated / (eigen + damping)
    self_score = jnp.sum(rotated * scaled, axis=(1, 2))
    mapped = jnp.einsum("qij,ai->qaj", scaled, basis_in, precision=high)
    mapped = jnp.einsum("qaj,bj->qab", mapped, basis_out, precision=high)
    return mapped, self_score


def kernel(
    n, pair, tiles, blk, docs, factor, out, got, docs_v, acc, mine, theirs, selfs,
    their_selfs, send_sem, recv_sem, doc_sem, ex_send, ex_recv,
):
    me = lax.axis_index("docs")
    core = lax.axis_index("mods")
    z = lax.div(me, pair)
    y = lax.rem(me, pair)
    depth = n // pair
    up, down = me + pair, me - pair
    beside = z * pair + (pair - 1 - y)
    has_up, has_down = z < depth - 1, z > 0
    q = blk.shape[0]
    wide = blk.shape[1]
    features = docs.shape[1]
    third = features // 3
    edges = (0, third, 2 * third, 2 * third + third // 4 * 3, features)
    chunks = len(edges) - 1
    tile = docs.shape[0] // tiles

    def load(c):
        cols = pl.ds(edges[c], edges[c + 1] - edges[c])
        return pltpu.make_async_copy(docs.at[:, cols], docs_v.at[:, cols], doc_sem.at[c])

    for c in range(chunks):
        load(c).start()

    barrier = pltpu.get_barrier_semaphore()
    for yes, to in ((has_up, up), (has_down, down)):

        @pl.when(yes)
        def _(to=to):
            pl.semaphore_signal(barrier, inc=1, device_id={"docs": to}, device_id_type=MESH)

    if pair > 1:
        pl.semaphore_signal(barrier, inc=1, device_id={"docs": beside}, device_id_type=MESH)
    pl.semaphore_signal(barrier, inc=1, device_id={"mods": 1 - core}, device_id_type=MESH)
    peers = 2 if pair > 1 else 1
    line_peers = has_up.astype(jnp.int32) + has_down.astype(jnp.int32)
    pl.semaphore_wait(barrier, peers + line_peers)

    both = pair > 1

    def piece(source, k):
        c = k // 2
        start, stop = edges[c], edges[c + 1] if c < chunks - 1 else wide
        cut = stop - (stop - start) * 5 // 32 // 128 * 128 if both else stop
        start, stop = (start, cut) if k % 2 == 0 else (cut, stop)
        return (pl.ds(pl.multiple_of(source * q, q), q), pl.ds(start, stop - start))

    def copy(way, source, k, own=False):
        rows, cols = piece(source, k)
        to = (up, down, beside)[way]
        return pltpu.make_async_remote_copy(
            src_ref=blk.at[:, cols] if own else got.at[rows, cols],
            dst_ref=got.at[rows, cols],
            send_sem=send_sem.at[way, source, k],
            recv_sem=recv_sem.at[source, k],
            device_id={"docs": to},
            device_id_type=MESH,
        )

    lines = ((has_up, 0), (has_down, 1))
    pending = []

    def act(one, first):
        if first:
            one.start()
        else:
            one.wait_send()

    def own_each(c, first):
        if both:
            act(copy(2, me, 2 * c + 1, True), first)
            act(copy(2, me, 2 * c, True), first)
        for yes, way in lines:

            @pl.when(yes)
            def _(way=way):
                act(copy(way, me, 2 * c, True), first)
                if both:
                    act(copy(way, me, 2 * c + 1, True), first)

    def beside_each(c, first):
        if both:
            if first:
                copy(2, beside, 2 * c + 1).wait_recv()
            for yes, way in lines:

                @pl.when(yes)
                def _(way=way):
                    act(copy(way, beside, 2 * c + 1), first)

    def line_each(c, first):
        beside_each(c, first)
        for d in range(1, depth):
            for (onward, way), here, by in zip(lines, (z >= d, z + d < depth), (-d, d)):

                @pl.when(here)
                def _(onward=onward, way=way, by=by):
                    moves = [(me + by * pair, 2 * c)]
                    if both:
                        moves += [(me + by * pair, 2 * c + 1), (beside + by * pair, 2 * c + 1)]
                    for source, k in moves:
                        if first:
                            copy(way, source, k).wait_recv()

                        @pl.when(onward)
                        def _(source=source, k=k):
                            act(copy(way, source, k), first)

                        if both and k % 2 == 0:
                            act(copy(2, source, k), first)

            if first and pending:
                pending.pop(0)()

    def beside_wait(c):
        if both:
            for level in range(depth):
                copy(2, level * pair + (pair - 1 - y), 2 * c).wait_recv()

    def product(c, t):
        rows = pl.ds(t * tile, tile)
        cols = pl.ds(edges[c], edges[c + 1] - edges[c])
        value = lax.dot_general(docs_v[rows, cols], got[:, cols], NT, preferred_element_type=f32)
        if c == 0:
            acc[rows, :] = value
            return value
        return acc[rows, :] + value

    def add(c, t):
        value = product(c, t)
        if c > 0:
            acc[pl.ds(t * tile, tile), :] = value

    for c in range(chunks):
        own_each(c, True)
    got[pl.ds(pl.multiple_of(me * q, q), q), :] = blk[...]
    for c in range(chunks):
        line_each(c, True)
        while pending:
            pending.pop(0)()
        if c >= 1:
            beside_wait(c - 1)
            load(c - 1).wait()
            pending.extend(functools.partial(add, c - 1, t) for t in range(tiles))
            pending.pop(0)()
    while pending:
        pending.pop(0)()

    last = chunks - 1
    beside_wait(last)
    load(last).wait()

    def swap(t):
        if t == tiles:
            src, dst = selfs, their_selfs
        else:
            rows = pl.ds(t * tile, tile)
            src, dst = mine.at[rows, :], theirs.at[rows, :]
        return pltpu.make_async_remote_copy(
            src_ref=src,
            dst_ref=dst,
            send_sem=ex_send.at[t],
            recv_sem=ex_recv.at[t],
            device_id={"mods": 1 - core},
            device_id_type=MESH,
        )

    lane = lax.broadcasted_iota(jnp.int32, (16, wide - features), 1)
    pick = jnp.where(lane < 2, 1.0, 0.0).astype(bf16)
    selfs[...] = lax.dot_general(
        pick, got[:, pl.ds(features, wide - features)], NT, preferred_element_type=f32
    )
    swap(tiles).start()
    for t in range(tiles):
        mine[pl.ds(t * tile, tile), :] = product(last, t).astype(bf16)
        swap(t).start()
    swap(tiles).wait()
    scale = lax.rsqrt(selfs[0:1, :] + their_selfs[0:1, :])
    for t in range(tiles):
        rows = pl.ds(t * tile, tile)
        swap(t).wait()
        total = mine[rows, :].astype(f32) + theirs[rows, :].astype(f32)
        out[rows, :] = total * scale * factor[rows, :]
    for c in range(chunks):
        own_each(c, False)
        line_each(c, False)


def gather_and_score(n, pair, block, docs, factor):
    q, wide = block.shape
    rows, features = docs.shape
    queries, tiles = n * q, 4
    vmem = pl.BlockSpec(memory_space=pltpu.VMEM)
    return pl.pallas_call(
        functools.partial(kernel, n, pair, tiles),
        out_shape=jax.ShapeDtypeStruct((rows, queries), f32),
        in_specs=[vmem, pl.BlockSpec(memory_space=pl.ANY), vmem],
        out_specs=vmem,
        scratch_shapes=[
            pltpu.VMEM((queries, wide), bf16),
            pltpu.VMEM((rows, features), bf16),
            pltpu.VMEM((rows, queries), f32),
            pltpu.VMEM((rows, queries), bf16),
            pltpu.VMEM((rows, queries), bf16),
            pltpu.VMEM((16, queries), f32),
            pltpu.VMEM((16, queries), f32),
            pltpu.SemaphoreType.DMA((3, n, 8)),
            pltpu.SemaphoreType.DMA((n, 8)),
            pltpu.SemaphoreType.DMA((4,)),
            pltpu.SemaphoreType.DMA((tiles + 1,)),
            pltpu.SemaphoreType.DMA((tiles + 1,)),
        ],
        compiler_params=pltpu.CompilerParams(
            collective_id=0, has_side_effects=True, vmem_limit_bytes=52 << 20
        ),
        cost_estimate=pl.CostEstimate(
            flops=2 * rows * features * queries,
            bytes_accessed=2 * rows * features,
            transcendentals=0,
        ),
    )(block, docs, factor)


def shards(n, pair, doc_grads, query_grads, basis_in, basis_out, eigen, token_counts):
    queries_here = query_grads.shape[0]
    mods_here = basis_in.shape[0]
    width = basis_in.shape[1]
    size = width * width
    self_part = jnp.zeros((queries_here,), f32)
    blocks = []
    for m in range(mods_here):
        gradient = query_grads[:, m * size : (m + 1) * size]
        gradient = gradient.reshape(queries_here, width, width).astype(f32)
        mapped, self_m = precondition(gradient, basis_in[m], basis_out[m], eigen[m])
        self_part = self_part + self_m
        blocks.append(mapped.reshape(queries_here, size).astype(bf16))
    upper = self_part.astype(bf16)
    lower = (self_part - upper.astype(f32)).astype(bf16)
    blocks.append(jnp.pad(jnp.stack([upper, lower], axis=1), ((0, 0), (0, 126))))
    block = jnp.concatenate(blocks, axis=1)
    factor = (ref_tokens / token_counts.astype(f32))[:, None]
    return gather_and_score(n, pair, block, doc_grads, factor)


def solution(mesh):
    n = mesh.shape["docs"]
    pair = 2 if mesh.shape["groups"] == 2 and n % 2 == 0 else 1
    in_specs = (
        P(("groups", "docs"), "mods"),
        P(("groups", "docs"), "mods"),
        P("mods", None, None),
        P("mods", None, None),
        P("mods", None, None),
        P(("groups", "docs")),
    )
    out_specs = P(("groups", "docs"), None)
    body = functools.partial(shards, n, pair)
    return jax.shard_map(body, mesh=mesh, in_specs=in_specs, out_specs=out_specs, check_vma=False)
```

```python
import functools

import jax
import jax.numpy as jnp
from jax import lax
from jax.experimental import pallas as pl
from jax.experimental.pallas import tpu as pltpu
from jax.sharding import PartitionSpec as P

ref_tokens = 1024.0
bf16, f32 = jnp.bfloat16, jnp.float32
MESH = pl.DeviceIdType.MESH
NT = (((1,), (1,)), ((), ()))


def precondition(gradient, basis_in, basis_out, eigen):
    high = lax.Precision.HIGH
    rotated = jnp.einsum("qab,bj->qaj", gradient, basis_out, precision=high)
    rotated = jnp.einsum("qaj,ai->qij", rotated, basis_in, precision=high)
    damping = 0.1 * jnp.mean(eigen)
    scaled = rotated / (eigen + damping)
    self_score = jnp.sum(rotated * scaled, axis=(1, 2))
    mapped = jnp.einsum("qij,ai->qaj", scaled, basis_in, precision=high)
    mapped = jnp.einsum("qaj,bj->qab", mapped, basis_out, precision=high)
    return mapped, self_score


def kernel(
    n, pair, tiles, blk, docs, out, self_out, got, docs_v, acc, mine, theirs, selfs,
    their_selfs, send_sem, recv_sem, doc_sem, ex_send, ex_recv,
):
    me = lax.axis_index("docs")
    core = lax.axis_index("mods")
    z = lax.div(me, pair)
    y = lax.rem(me, pair)
    depth = n // pair
    up, down = me + pair, me - pair
    beside = z * pair + (pair - 1 - y)
    has_up, has_down = z < depth - 1, z > 0
    q = blk.shape[0]
    wide = blk.shape[1]
    features = docs.shape[1]
    third = features // 3
    edges = (0, third, 2 * third, 2 * third + third // 4 * 3, features)
    chunks = len(edges) - 1
    tile = docs.shape[0] // tiles

    def load(c):
        cols = pl.ds(edges[c], edges[c + 1] - edges[c])
        return pltpu.make_async_copy(docs.at[:, cols], docs_v.at[:, cols], doc_sem.at[c])

    for c in range(chunks):
        load(c).start()

    barrier = pltpu.get_barrier_semaphore()
    for yes, to in ((has_up, up), (has_down, down)):

        @pl.when(yes)
        def _(to=to):
            pl.semaphore_signal(barrier, inc=1, device_id={"docs": to}, device_id_type=MESH)

    if pair > 1:
        pl.semaphore_signal(barrier, inc=1, device_id={"docs": beside}, device_id_type=MESH)
    pl.semaphore_signal(barrier, inc=1, device_id={"mods": 1 - core}, device_id_type=MESH)
    peers = 2 if pair > 1 else 1
    line_peers = has_up.astype(jnp.int32) + has_down.astype(jnp.int32)
    pl.semaphore_wait(barrier, peers + line_peers)

    both = pair > 1

    def piece(source, k):
        c = k // 2
        start, stop = edges[c], edges[c + 1] if c < chunks - 1 else wide
        cut = stop - (stop - start) * 5 // 32 // 128 * 128 if both else stop
        start, stop = (start, cut) if k % 2 == 0 else (cut, stop)
        return (pl.ds(pl.multiple_of(source * q, q), q), pl.ds(start, stop - start))

    def copy(way, source, k, own=False):
        rows, cols = piece(source, k)
        to = (up, down, beside)[way]
        return pltpu.make_async_remote_copy(
            src_ref=blk.at[:, cols] if own else got.at[rows, cols],
            dst_ref=got.at[rows, cols],
            send_sem=send_sem.at[way, source, k],
            recv_sem=recv_sem.at[source, k],
            device_id={"docs": to},
            device_id_type=MESH,
        )

    lines = ((has_up, 0), (has_down, 1))

    def act(one, first):
        if first:
            one.start()
        else:
            one.wait_send()

    def own_each(c, first):
        if both:
            act(copy(2, me, 2 * c + 1, True), first)
            act(copy(2, me, 2 * c, True), first)
        for yes, way in lines:

            @pl.when(yes)
            def _(way=way):
                act(copy(way, me, 2 * c, True), first)
                if both:
                    act(copy(way, me, 2 * c + 1, True), first)

    def beside_each(c, first):
        if both:
            if first:
                copy(2, beside, 2 * c + 1).wait_recv()
            for yes, way in lines:

                @pl.when(yes)
                def _(way=way):
                    act(copy(way, beside, 2 * c + 1), first)

    def line_each(c, first):
        beside_each(c, first)
        for d in range(1, depth):
            for (onward, way), here, by in zip(lines, (z >= d, z + d < depth), (-d, d)):

                @pl.when(here)
                def _(onward=onward, way=way, by=by):
                    moves = [(me + by * pair, 2 * c)]
                    if both:
                        moves += [(me + by * pair, 2 * c + 1), (beside + by * pair, 2 * c + 1)]
                    for source, k in moves:
                        if first:
                            copy(way, source, k).wait_recv()

                        @pl.when(onward)
                        def _(source=source, k=k):
                            act(copy(way, source, k), first)

                        if both and k % 2 == 0:
                            act(copy(2, source, k), first)

    def beside_wait(c):
        if both:
            for level in range(depth):
                copy(2, level * pair + (pair - 1 - y), 2 * c).wait_recv()

    def product(c, t):
        rows = pl.ds(t * tile, tile)
        cols = pl.ds(edges[c], edges[c + 1] - edges[c])
        value = lax.dot_general(docs_v[rows, cols], got[:, cols], NT, preferred_element_type=f32)
        if c == 0:
            acc[rows, :] = value
            return value
        return acc[rows, :] + value

    for c in range(min(2, chunks)):
        own_each(c, True)
    got[pl.ds(pl.multiple_of(me * q, q), q), :] = blk[...]
    for c in range(chunks):
        line_each(c, True)
        if c + 2 < chunks:
            own_each(c + 2, True)
        if c >= 1:
            beside_wait(c - 1)
            load(c - 1).wait()
            for t in range(tiles):
                value = product(c - 1, t)
                if c > 1:
                    acc[pl.ds(t * tile, tile), :] = value

    last = chunks - 1
    beside_wait(last)
    load(last).wait()

    def swap(t):
        if t == tiles:
            src, dst = selfs, their_selfs
        else:
            rows = pl.ds(t * tile, tile)
            src, dst = mine.at[rows, :], theirs.at[rows, :]
        return pltpu.make_async_remote_copy(
            src_ref=src,
            dst_ref=dst,
            send_sem=ex_send.at[t],
            recv_sem=ex_recv.at[t],
            device_id={"mods": 1 - core},
            device_id_type=MESH,
        )

    lane = lax.broadcasted_iota(jnp.int32, (16, wide - features), 1)
    pick = jnp.where(lane < 2, 1.0, 0.0).astype(bf16)
    selfs[...] = lax.dot_general(
        pick, got[:, pl.ds(features, wide - features)], NT, preferred_element_type=f32
    )
    swap(tiles).start()
    for t in range(tiles):
        mine[pl.ds(t * tile, tile), :] = product(last, t).astype(bf16)
        swap(t).start()
    swap(tiles).wait()
    self_out[...] = selfs[...] + their_selfs[...]
    for t in range(tiles):
        rows = pl.ds(t * tile, tile)
        swap(t).wait()
        out[rows, :] = mine[rows, :].astype(f32) + theirs[rows, :].astype(f32)
    for c in range(chunks):
        own_each(c, False)
        line_each(c, False)


def gather_and_score(n, pair, block, docs):
    q, wide = block.shape
    rows, features = docs.shape
    queries, tiles = n * q, 4
    vmem = pl.BlockSpec(memory_space=pltpu.VMEM)
    return pl.pallas_call(
        functools.partial(kernel, n, pair, tiles),
        out_shape=(
            jax.ShapeDtypeStruct((rows, queries), f32),
            jax.ShapeDtypeStruct((16, queries), f32),
        ),
        in_specs=[vmem, pl.BlockSpec(memory_space=pl.ANY)],
        out_specs=(vmem, vmem),
        scratch_shapes=[
            pltpu.VMEM((queries, wide), bf16),
            pltpu.VMEM((rows, features), bf16),
            pltpu.VMEM((rows, queries), f32),
            pltpu.VMEM((rows, queries), bf16),
            pltpu.VMEM((rows, queries), bf16),
            pltpu.VMEM((16, queries), f32),
            pltpu.VMEM((16, queries), f32),
            pltpu.SemaphoreType.DMA((3, n, 8)),
            pltpu.SemaphoreType.DMA((n, 8)),
            pltpu.SemaphoreType.DMA((4,)),
            pltpu.SemaphoreType.DMA((tiles + 1,)),
            pltpu.SemaphoreType.DMA((tiles + 1,)),
        ],
        compiler_params=pltpu.CompilerParams(
            collective_id=0, has_side_effects=True, vmem_limit_bytes=52 << 20
        ),
        cost_estimate=pl.CostEstimate(
            flops=2 * rows * features * queries,
            bytes_accessed=2 * rows * features,
            transcendentals=0,
        ),
    )(block, docs)


def shards(n, pair, doc_grads, query_grads, basis_in, basis_out, eigen, token_counts):
    queries_here = query_grads.shape[0]
    mods_here = basis_in.shape[0]
    width = basis_in.shape[1]
    size = width * width
    self_part = jnp.zeros((queries_here,), f32)
    blocks = []
    for m in range(mods_here):
        gradient = query_grads[:, m * size : (m + 1) * size]
        gradient = gradient.reshape(queries_here, width, width).astype(f32)
        mapped, self_m = precondition(gradient, basis_in[m], basis_out[m], eigen[m])
        self_part = self_part + self_m
        blocks.append(mapped.reshape(queries_here, size).astype(bf16))
    upper = self_part.astype(bf16)
    lower = (self_part - upper.astype(f32)).astype(bf16)
    blocks.append(jnp.pad(jnp.stack([upper, lower], axis=1), ((0, 0), (0, 126))))
    block = jnp.concatenate(blocks, axis=1)
    totals, self_terms = gather_and_score(n, pair, block, doc_grads)
    factor = ref_tokens / token_counts.astype(f32)
    return totals * lax.rsqrt(self_terms[0])[None, :] * factor[:, None]


def solution(mesh):
    n = mesh.shape["docs"]
    pair = 2 if mesh.shape["groups"] == 2 and n % 2 == 0 else 1
    in_specs = (
        P(("groups", "docs"), "mods"),
        P(("groups", "docs"), "mods"),
        P("mods", None, None),
        P("mods", None, None),
        P("mods", None, None),
        P(("groups", "docs")),
    )
    out_specs = P(("groups", "docs"), None)
    body = functools.partial(shards, n, pair)
    return jax.shard_map(body, mesh=mesh, in_specs=in_specs, out_specs=out_specs, check_vma=False)
```

```python
import functools

import jax
import jax.numpy as jnp
from jax import lax
from jax.experimental import pallas as pl
from jax.experimental.pallas import tpu as pltpu
from jax.sharding import PartitionSpec as P

ref_tokens = 1024.0
bf16, f32 = jnp.bfloat16, jnp.float32
MESH = pl.DeviceIdType.MESH
NT = (((1,), (1,)), ((), ()))


def precondition(gradient, basis_in, basis_out, eigen):
    high = lax.Precision.HIGH
    rotated = jnp.einsum("qab,bj->qaj", gradient, basis_out, precision=high)
    rotated = jnp.einsum("qaj,ai->qij", rotated, basis_in, precision=high)
    damping = 0.1 * jnp.mean(eigen)
    scaled = rotated / (eigen + damping)
    self_score = jnp.sum(rotated * scaled, axis=(1, 2))
    mapped = jnp.einsum("qij,ai->qaj", scaled, basis_in, precision=high)
    mapped = jnp.einsum("qaj,bj->qab", mapped, basis_out, precision=high)
    return mapped, self_score


def kernel(
    n, pair, tiles, blk, docs, factor, out, got, docs_v, acc, mine, theirs, selfs,
    their_selfs, send_sem, recv_sem, doc_sem, ex_send, ex_recv,
):
    me = lax.axis_index("docs")
    core = lax.axis_index("mods")
    z = lax.div(me, pair)
    y = lax.rem(me, pair)
    depth = n // pair
    up, down = me + pair, me - pair
    beside = z * pair + (pair - 1 - y)
    has_up, has_down = z < depth - 1, z > 0
    q = blk.shape[0]
    wide = blk.shape[1]
    features = docs.shape[1]
    fine = features // 96
    edges = tuple(fine * step for step in (0, 24, 48, 72, 88, 96))
    chunks = len(edges) - 1
    tile = docs.shape[0] // tiles

    def load(c):
        cols = pl.ds(edges[c], edges[c + 1] - edges[c])
        return pltpu.make_async_copy(docs.at[:, cols], docs_v.at[:, cols], doc_sem.at[c])

    for c in range(chunks):
        load(c).start()

    barrier = pltpu.get_barrier_semaphore()
    for yes, to in ((has_up, up), (has_down, down)):

        @pl.when(yes)
        def _(to=to):
            pl.semaphore_signal(barrier, inc=1, device_id={"docs": to}, device_id_type=MESH)

    if pair > 1:
        pl.semaphore_signal(barrier, inc=1, device_id={"docs": beside}, device_id_type=MESH)
    pl.semaphore_signal(barrier, inc=1, device_id={"mods": 1 - core}, device_id_type=MESH)
    peers = 2 if pair > 1 else 1
    line_peers = has_up.astype(jnp.int32) + has_down.astype(jnp.int32)
    pl.semaphore_wait(barrier, peers + line_peers)

    both = pair > 1

    def piece(source, k):
        c = k // 2
        start, stop = edges[c], edges[c + 1] if c < chunks - 1 else wide
        cut = stop - (stop - start) * 5 // 32 // 128 * 128 if both else stop
        start, stop = (start, cut) if k % 2 == 0 else (cut, stop)
        return (pl.ds(pl.multiple_of(source * q, q), q), pl.ds(start, stop - start))

    def copy(way, source, k, own=False):
        rows, cols = piece(source, k)
        to = (up, down, beside)[way]
        return pltpu.make_async_remote_copy(
            src_ref=blk.at[:, cols] if own else got.at[rows, cols],
            dst_ref=got.at[rows, cols],
            send_sem=send_sem.at[way, source, k],
            recv_sem=recv_sem.at[source, k],
            device_id={"docs": to},
            device_id_type=MESH,
        )

    lines = ((has_up, 0), (has_down, 1))

    def act(one, first):
        if first:
            one.start()
        else:
            one.wait_send()

    def own_each(c, first):
        if both:
            act(copy(2, me, 2 * c + 1, True), first)
            act(copy(2, me, 2 * c, True), first)
        for yes, way in lines:

            @pl.when(yes)
            def _(way=way):
                act(copy(way, me, 2 * c, True), first)
                if both:
                    act(copy(way, me, 2 * c + 1, True), first)

    def beside_each(c, first):
        if both:
            if first:
                copy(2, beside, 2 * c + 1).wait_recv()
            for yes, way in lines:

                @pl.when(yes)
                def _(way=way):
                    act(copy(way, beside, 2 * c + 1), first)

    def line_each(c, first):
        beside_each(c, first)
        for d in range(1, depth):
            for (onward, way), here, by in zip(lines, (z >= d, z + d < depth), (-d, d)):

                @pl.when(here)
                def _(onward=onward, way=way, by=by):
                    moves = [(me + by * pair, 2 * c)]
                    if both:
                        moves += [(me + by * pair, 2 * c + 1), (beside + by * pair, 2 * c + 1)]
                    for source, k in moves:
                        if first:
                            copy(way, source, k).wait_recv()

                        @pl.when(onward)
                        def _(source=source, k=k):
                            act(copy(way, source, k), first)

                        if both and k % 2 == 0:
                            act(copy(2, source, k), first)

    def beside_wait(c):
        if both:
            for level in range(depth):
                copy(2, level * pair + (pair - 1 - y), 2 * c).wait_recv()

    def product(c, t):
        rows = pl.ds(t * tile, tile)
        cols = pl.ds(edges[c], edges[c + 1] - edges[c])
        value = lax.dot_general(docs_v[rows, cols], got[:, cols], NT, preferred_element_type=f32)
        if c == 0:
            acc[rows, :] = value
            return value
        return acc[rows, :] + value

    for c in range(min(2, chunks)):
        own_each(c, True)
    got[pl.ds(pl.multiple_of(me * q, q), q), :] = blk[...]
    for c in range(chunks):
        line_each(c, True)
        if c + 2 < chunks:
            own_each(c + 2, True)
        if c >= 1:
            beside_wait(c - 1)
            load(c - 1).wait()
            for t in range(tiles):
                value = product(c - 1, t)
                if c > 1:
                    acc[pl.ds(t * tile, tile), :] = value

    last = chunks - 1
    beside_wait(last)
    load(last).wait()

    def swap(t):
        if t == tiles:
            src, dst = selfs, their_selfs
        else:
            rows = pl.ds(t * tile, tile)
            src, dst = mine.at[rows, :], theirs.at[rows, :]
        return pltpu.make_async_remote_copy(
            src_ref=src,
            dst_ref=dst,
            send_sem=ex_send.at[t],
            recv_sem=ex_recv.at[t],
            device_id={"mods": 1 - core},
            device_id_type=MESH,
        )

    lane = lax.broadcasted_iota(jnp.int32, (16, wide - features), 1)
    pick = jnp.where(lane < 2, 1.0, 0.0).astype(bf16)
    selfs[...] = lax.dot_general(
        pick, got[:, pl.ds(features, wide - features)], NT, preferred_element_type=f32
    )
    swap(tiles).start()
    for t in range(tiles):
        mine[pl.ds(t * tile, tile), :] = product(last, t).astype(bf16)
        swap(t).start()
    swap(tiles).wait()
    scale = lax.rsqrt(selfs[0:1, :] + their_selfs[0:1, :])
    for t in range(tiles):
        rows = pl.ds(t * tile, tile)
        swap(t).wait()
        total = mine[rows, :].astype(f32) + theirs[rows, :].astype(f32)
        out[rows, :] = total * scale * factor[rows, :]
    for c in range(chunks):
        own_each(c, False)
        line_each(c, False)


def gather_and_score(n, pair, block, docs, factor):
    q, wide = block.shape
    rows, features = docs.shape
    queries, tiles = n * q, 4
    vmem = pl.BlockSpec(memory_space=pltpu.VMEM)
    return pl.pallas_call(
        functools.partial(kernel, n, pair, tiles),
        out_shape=jax.ShapeDtypeStruct((rows, queries), f32),
        in_specs=[vmem, pl.BlockSpec(memory_space=pl.ANY), vmem],
        out_specs=vmem,
        scratch_shapes=[
            pltpu.VMEM((queries, wide), bf16),
            pltpu.VMEM((rows, features), bf16),
            pltpu.VMEM((rows, queries), f32),
            pltpu.VMEM((rows, queries), bf16),
            pltpu.VMEM((rows, queries), bf16),
            pltpu.VMEM((16, queries), f32),
            pltpu.VMEM((16, queries), f32),
            pltpu.SemaphoreType.DMA((3, n, 10)),
            pltpu.SemaphoreType.DMA((n, 10)),
            pltpu.SemaphoreType.DMA((5,)),
            pltpu.SemaphoreType.DMA((tiles + 1,)),
            pltpu.SemaphoreType.DMA((tiles + 1,)),
        ],
        compiler_params=pltpu.CompilerParams(
            collective_id=0, has_side_effects=True, vmem_limit_bytes=52 << 20
        ),
        cost_estimate=pl.CostEstimate(
            flops=2 * rows * features * queries,
            bytes_accessed=2 * rows * features,
            transcendentals=0,
        ),
    )(block, docs, factor)


def shards(n, pair, doc_grads, query_grads, basis_in, basis_out, eigen, token_counts):
    queries_here = query_grads.shape[0]
    mods_here = basis_in.shape[0]
    width = basis_in.shape[1]
    size = width * width
    self_part = jnp.zeros((queries_here,), f32)
    blocks = []
    for m in range(mods_here):
        gradient = query_grads[:, m * size : (m + 1) * size]
        gradient = gradient.reshape(queries_here, width, width).astype(f32)
        mapped, self_m = precondition(gradient, basis_in[m], basis_out[m], eigen[m])
        self_part = self_part + self_m
        blocks.append(mapped.reshape(queries_here, size).astype(bf16))
    upper = self_part.astype(bf16)
    lower = (self_part - upper.astype(f32)).astype(bf16)
    blocks.append(jnp.pad(jnp.stack([upper, lower], axis=1), ((0, 0), (0, 126))))
    block = jnp.concatenate(blocks, axis=1)
    factor = (ref_tokens / token_counts.astype(f32))[:, None]
    return gather_and_score(n, pair, block, doc_grads, factor)


def solution(mesh):
    n = mesh.shape["docs"]
    pair = 2 if mesh.shape["groups"] == 2 and n % 2 == 0 else 1
    in_specs = (
        P(("groups", "docs"), "mods"),
        P(("groups", "docs"), "mods"),
        P("mods", None, None),
        P("mods", None, None),
        P("mods", None, None),
        P(("groups", "docs")),
    )
    out_specs = P(("groups", "docs"), None)
    body = functools.partial(shards, n, pair)
    return jax.shard_map(body, mesh=mesh, in_specs=in_specs, out_specs=out_specs, check_vma=False)
```
